768 devices in a mesh: pair: 48 (over y, z_lo), virt: 16 (over x, z_hi, core).
Axes of the slice: x: 4, y: 8, z: 12 (z_hi: 2, z_lo: 6; z = z_hi * 6 + z_lo), core: 2. Of those that a mesh axis runs over, the one named last changes fastest.
Arguments:
- amplitudes: bfloat16 [96, 2048, 2048], P('pair', 'virt'), may hold values from -6 to 6
- tile_mask: int32 [96, 32, 32], P('pair', 'virt'), may hold values 0 or 1
- cycle_integral: bfloat16 [2048, 2048], P('virt'), may hold values from -0.125 to 0.125
Outputs:
- residual: bfloat16 [96, 2048, 2048], P('pair', 'virt')
The draws below stay inside these ranges and needn't reach their ends.
All inputs are finite; a program needn't handle non-finite values. No bound on the sum of `tile_mask` on one device may be relied on, other than what follows from the above.
Results may differ from the reference program's by a relative error of at most 0.0051.
Values may be sent and summed in bfloat16 or wider, within the bound.
No kernel may reach another device: no remote copies, remote signals or barrier semaphores. Data moves between devices by JAX's collectives and lax.ppermute only.
A program may use at most 32 MiB of HBM per device.

```python
import jax
import jax.numpy as jnp
from jax import lax

TILE = 64
NV = 2048
NT = 32
PAIRS = 96


def place_ends(drawn, rng, smallest, high):
    shape = drawn.shape
    index_at = [jax.random.randint(jax.random.fold_in(rng, axis), (), 0, shape[axis]) for axis in range(len(shape))]
    drawn = drawn.at[tuple(index_at)].set(smallest)
    longest = shape.index(max(shape))
    index_at[longest] = (index_at[longest] + 1) % shape[longest]
    return drawn.at[tuple(index_at)].set(high)


def levels(rng, shape, cuts, least, top_value):
    factor_of, own = 1.0, jax.random.fold_in(rng, 6)
    for dim, parts in cuts:
        draws = jnp.exp(jax.random.uniform(jax.random.fold_in(own, dim), (parts,), jnp.float32, least / len(cuts), top_value / len(cuts)))
        factor_of = factor_of * jnp.repeat(draws, shape[dim] // parts).reshape([-1 if axis == dim else 1 for axis in range(len(shape))])
    return factor_of


def noise(stream_key, shape, deviation, bound, split=(), dtype=jnp.bfloat16):
    entries = deviation * jax.random.normal(stream_key, shape, jnp.float32)
    if split:
        entries = entries * levels(stream_key, shape, split, -0.22, 0.18)
    return jnp.clip(entries, -bound, bound).astype(dtype)


def setup_inputs(seed: int = 0) -> dict:
    streams_of = jax.random.split(jax.random.key(seed), 4)
    return {
        "amplitudes": noise(streams_of[0], (PAIRS, NV, NV), 1.0, 6.0, ((0, 48), (1, 16))),
        "tile_mask": place_ends((jax.random.randint(streams_of[1], (PAIRS, NT, NT), 0, 2) < 1).astype(jnp.int32), jax.random.fold_in(streams_of[1], 1), 0, 1),
        "cycle_integral": noise(streams_of[2], (NV, NV), NV ** -0.5, 0.125, ((0, 16),)),
    }


def reference(amplitudes, tile_mask, cycle_integral):
    def one_pair(args):
        block, mask = args
        full = jnp.repeat(jnp.repeat(mask, TILE, axis=0), TILE, axis=1).astype(jnp.bfloat16)
        masked = block * full
        return jnp.dot(masked, cycle_integral, preferred_element_type=jnp.float32).astype(jnp.bfloat16)

    cycle = lax.map(one_pair, (amplitudes, tile_mask))
    mirrored = jnp.roll(cycle, -(PAIRS // 2), axis=0)

    def symmetrize(args):
        own, other = args
        return (own.astype(jnp.float32) + other.T.astype(jnp.float32)).astype(jnp.bfloat16)

    return lax.map(symmetrize, (cycle, mirrored))
```

```python
import functools

import jax
import jax.numpy as jnp
from jax import lax
from jax.experimental import pallas as pl
from jax.experimental.pallas import tpu as pltpu
from jax.sharding import Mesh, PartitionSpec as P

TILE = 64
X, ZH, C, Y, ZL = 4, 2, 2, 8, 6
D = X * ZH
ROWS = 128
W = 2 * ROWS
NV = D * W
HALVES = 1
PART = ROWS // HALVES
N = D * PART

VMEM = pl.BlockSpec(memory_space=pltpu.VMEM)
SMEM = pl.BlockSpec(memory_space=pltpu.SMEM)
LIMIT = 40 * 1024 * 1024


def params():
    return pltpu.CompilerParams(vmem_limit_bytes=LIMIT)


def mask_kernel(zh_ref, amp_ref, rows_ref, out_ref):
    zh = zh_ref[0]
    tiles = rows_ref.shape[2]
    spread = (
        lax.broadcasted_iota(jnp.int32, (tiles, NV), 1) // TILE
        == lax.broadcasted_iota(jnp.int32, (tiles, NV), 0)
    ).astype(jnp.bfloat16)
    for pair in range(2):
        full = jnp.dot(rows_ref[pair], spread, preferred_element_type=jnp.float32)
        masked = amp_ref[pair] * full.astype(jnp.bfloat16)
        for d in range(D):
            x, z = divmod(d, ZH)
            to = x * W + jnp.where(zh == z, 0, NV // 2)
            out_ref[pair, :, pl.ds(pl.multiple_of(to, W), W)] = masked[:, d * W : (d + 1) * W]


def mask_amplitudes(zh, amplitudes, tile_mask):
    rows = jnp.repeat(tile_mask.astype(jnp.bfloat16), TILE, axis=1)
    return pl.pallas_call(
        mask_kernel,
        out_shape=jax.ShapeDtypeStruct(amplitudes.shape, jnp.bfloat16),
        in_specs=[SMEM, VMEM, VMEM],
        out_specs=VMEM,
        compiler_params=params(),
        cost_estimate=pl.CostEstimate(flops=4 * ROWS * 32 * NV, bytes_accessed=2 << 20, transcendentals=0),
    )(zh, amplitudes, rows)


def product(mine_ref, theirs_ref, own_ref, other_ref):
    m = jnp.concatenate([mine_ref[0], mine_ref[1], theirs_ref[0], theirs_ref[1]], axis=0)
    half = NV // 2
    own = own_ref[...].reshape(half, own_ref.shape[-1])
    other = other_ref[...].reshape(half, other_ref.shape[-1])
    return jnp.dot(m[:, :half], own, preferred_element_type=jnp.float32) + jnp.dot(
        m[:, half:], other, preferred_element_type=jnp.float32
    )


def flip_kernel(core_ref, mine_ref, theirs_ref, own_ref, other_ref, out_ref):
    core = core_ref[0]
    found = product(mine_ref, theirs_ref, own_ref, other_ref)
    turned = found.T.astype(jnp.bfloat16)
    for d in range(out_ref.shape[0]):
        block = turned[d * PART : (d + 1) * PART]
        for pair in range(2):
            for source in range(2):
                at = (2 * source + pair) * ROWS
                to = jnp.where(core == source, 0, ROWS)
                out_ref[d, pair, :, pl.ds(pl.multiple_of(to, ROWS), ROWS)] = block[:, at : at + ROWS]


def matmul_specs(step):
    whole = pl.BlockSpec((2, ROWS, NV), lambda i: (0, 0, 0))
    part = pl.BlockSpec((X, W, step), lambda i: (0, 0, i))
    return [SMEM, whole, whole, part, part]


def flip_product(core, mine, theirs, own, other):
    step = 256
    return pl.pallas_call(
        flip_kernel,
        grid=(N // step,),
        out_shape=jax.ShapeDtypeStruct((D, 2, PART, W), jnp.bfloat16),
        in_specs=matmul_specs(step),
        out_specs=pl.BlockSpec((step // PART, 2, PART, W), lambda i: (i, 0, 0, 0)),
        compiler_params=params(),
        cost_estimate=pl.CostEstimate(flops=2 * 512 * NV * N, bytes_accessed=(2 << 20) + NV * N * 2, transcendentals=0),
    )(core, mine, theirs, own, other)


def own_kernel(core_ref, mine_ref, theirs_ref, own_ref, other_ref, keep_ref, send_ref):
    found = product(mine_ref, theirs_ref, own_ref, other_ref).astype(jnp.bfloat16)
    for pair in range(2):
        keep_ref[pair] = found[pair * ROWS : (pair + 1) * ROWS]
        send_ref[pair] = found[(2 + pair) * ROWS : (3 + pair) * ROWS]


def own_product(core, mine, theirs, own, other):
    step = 256
    out = jax.ShapeDtypeStruct((2, ROWS, N), jnp.bfloat16)
    spec = pl.BlockSpec((2, ROWS, step), lambda i: (0, 0, i))
    return pl.pallas_call(
        own_kernel,
        grid=(N // step,),
        out_shape=(out, out),
        in_specs=matmul_specs(step),
        out_specs=(spec, spec),
        compiler_params=params(),
        cost_estimate=pl.CostEstimate(flops=2 * 512 * NV * N, bytes_accessed=(3 << 20) + NV * N * 2, transcendentals=0),
    )(core, mine, theirs, own, other)


def sum_kernel(core_ref, *refs):
    keeps, gots, flips = refs[:HALVES], refs[HALVES : 2 * HALVES], refs[2 * HALVES : 3 * HALVES]
    out_ref = refs[3 * HALVES]
    core = core_ref[0]
    for d in range(D):
        turned = jnp.concatenate([f[d] for f in flips], axis=1).astype(jnp.float32)
        for source, parts in enumerate((keeps, gots)):
            at = jnp.where(core == source, 0, ROWS)
            cols = pl.ds(pl.multiple_of(d * W + at, ROWS), ROWS)
            straight = jnp.concatenate([k[:, :, d * PART : (d + 1) * PART] for k in parts], axis=2).astype(jnp.float32)
            low, high = turned[:, :, :ROWS], turned[:, :, ROWS:]
            out_ref[:, :, cols] = (straight + jnp.where(at == 0, low, high)).astype(jnp.bfloat16)


def symmetrized(core, keeps, gots, flips):
    return pl.pallas_call(
        sum_kernel,
        out_shape=jax.ShapeDtypeStruct((2, ROWS, NV), jnp.bfloat16),
        in_specs=[SMEM] + [VMEM] * (3 * HALVES),
        out_specs=VMEM,
        compiler_params=params(),
        cost_estimate=pl.CostEstimate(flops=2 * ROWS * NV, bytes_accessed=3 << 20, transcendentals=0),
    )(core, *keeps, *gots, *flips)


def swap(array, axis, size, by):
    return lax.ppermute(array, axis, [(i, (i + by) % size) for i in range(size)])


def spread_x(block):
    return lax.all_to_all(jnp.broadcast_to(block[None], (X, *block.shape)), "x", split_axis=0, concat_axis=0, tiled=True)


def local(amplitudes, tile_mask, cycle_integral):
    c = lax.axis_index("c")
    core = c.astype(jnp.int32).reshape(1)
    zh = lax.axis_index("zh").astype(jnp.int32).reshape(1)
    columns = cycle_integral.reshape(ROWS, D, C, HALVES, PART)
    mine, theirs = (
        lax.dynamic_index_in_dim(columns, i, axis=2, keepdims=False).transpose(2, 0, 1, 3).reshape(HALVES, ROWS, N)
        for i in (c, 1 - c)
    )
    got = swap(theirs, "c", C, 1)
    first = jnp.where(c == 0, mine, got)
    second = jnp.where(c == 0, got, mine)
    rows = jnp.concatenate([first, second], axis=1)
    crossed = [swap(rows[h], "zh", ZH, 1) for h in range(HALVES)]
    near = [spread_x(rows[h]) for h in range(HALVES)]
    far = [spread_x(crossed[h]) for h in range(HALVES)]

    masked = mask_amplitudes(zh, amplitudes, tile_mask)
    mirrored = swap(masked, "y", Y, Y // 2)
    masked_pair = swap(masked, "c", C, 1)
    mirrored_pair = swap(mirrored, "c", C, 1)

    flips = []
    for h in range(HALVES):
        out = flip_product(core, mirrored, mirrored_pair, near[h], far[h])
        flips.append(lax.all_to_all(out, ("x", "zh"), split_axis=0, concat_axis=0, tiled=True))
    keeps, gots = [], []
    for h in range(HALVES):
        keep, send = own_product(core, masked, masked_pair, near[h], far[h])
        keeps.append(keep)
        gots.append(swap(send, "c", C, 1))
    return symmetrized(core, keeps, gots, flips)


def solution(mesh):
    split = Mesh(mesh.devices.reshape(Y, ZL, X, ZH, C), ("y", "zl", "x", "zh", "c"))
    pair, virt = ("y", "zl"), ("x", "zh", "c")
    return jax.shard_map(
        local,
        mesh=split,
        in_specs=(P(pair, virt, None), P(pair, virt, None), P(virt, None)),
        out_specs=P(pair, virt, None),
        check_vma=False,
    )
```

```python
import functools

import jax
import jax.numpy as jnp
from jax import lax
from jax.experimental import pallas as pl
from jax.experimental.pallas import tpu as pltpu
from jax.sharding import Mesh, PartitionSpec as P

TILE = 64
X, ZH, C, Y, ZL = 4, 2, 2, 8, 6
D = X * ZH
ROWS = 128
W = C * ROWS
NV = D * W
WIDE = ZH * W
PARTS = 2

VMEM = pl.BlockSpec(memory_space=pltpu.VMEM)
SMEM = pl.BlockSpec(memory_space=pltpu.SMEM)
LIMIT = 16 * 1024 * 1024


def call(kernel, out_shape, *operands, flops=0):
    many = isinstance(out_shape, tuple)
    return pl.pallas_call(
        kernel,
        out_shape=out_shape,
        in_specs=[SMEM] + [VMEM] * (len(operands) - 1),
        out_specs=(VMEM,) * len(out_shape) if many else VMEM,
        compiler_params=pltpu.CompilerParams(vmem_limit_bytes=LIMIT),
        cost_estimate=pl.CostEstimate(flops=flops, bytes_accessed=0, transcendentals=0),
    )(*operands)


def shaped(*shape):
    return jax.ShapeDtypeStruct(shape, jnp.bfloat16)


def lanes(start, size):
    return pl.ds(pl.multiple_of(start, ROWS), size)


def first_kernel(place_ref, x_ref, amp_ref, mask_ref, sent_ref, *out_refs):
    for d in range(D):
        x = d // ZH
        sent_ref[d] = x_ref[:, x * WIDE : (x + 1) * WIDE]
    core = place_ref[2]
    blocks, tiles = mask_ref.shape[1:]
    spread = (
        lax.broadcasted_iota(jnp.int32, (tiles, NV), 1) // TILE
        == lax.broadcasted_iota(jnp.int32, (tiles, NV), 0)
    ).astype(jnp.bfloat16)
    for pair in range(2):
        rows = [
            jnp.broadcast_to(mask_ref[pair, b : b + 1, :].astype(jnp.float32), (TILE, tiles))
            for b in range(blocks)
        ]
        full = jnp.dot(
            jnp.concatenate(rows, axis=0).astype(jnp.bfloat16), spread, preferred_element_type=jnp.float32
        )
        masked = amp_ref[pair] * full.astype(jnp.bfloat16)
        for d in range(D):
            for number in range(C):
                at = (d * C + number) * ROWS
                to = jnp.where(core == number, 0, NV // 2) + d * ROWS
                out_refs[pair][:, lanes(to, ROWS)] = masked[:, at : at + ROWS]


def product_kernel(part, place_ref, mark_ref, own_ref, other_ref, *refs):
    blocks, (same_ref, cross_ref) = refs[: 2 * X], refs[-2:]
    zh, core = place_ref[1], place_ref[2]
    cols = lanes(lax.rem(zh + part, ZH) * W, W)
    x = jnp.concatenate([r[:, :, cols].reshape(NV // 2, W) for r in (own_ref, other_ref)], axis=0)
    if part:
        straight_refs = [refs[2 * X].at[dx] for dx in range(X)]
    else:
        straight_refs = [r.at[0] for r in refs[2 * X + 1 : 3 * X + 1]]
        for dx in range(X):
            refs[2 * X + 1 + dx][1] = refs[2 * X][dx]
    for pair in range(2):
        rows = jnp.concatenate([r[...] for r in blocks[pair * X : (pair + 1) * X]], axis=0)
        found = jnp.dot(rows, x, preferred_element_type=jnp.float32)
        turned = found.T.astype(jnp.bfloat16)
        low, high = turned[:ROWS], turned[ROWS:]
        same_ref[pair] = jnp.where(core == 0, low, high)
        cross_ref[pair] = jnp.where(core == 0, high, low)
        found = found.astype(jnp.bfloat16)
        for dx in range(X):
            straight_refs[dx][pair] = found[dx * ROWS : (dx + 1) * ROWS]


def product(part, place, mark, own, other, blocks, *earlier):
    flipped = shaped(2, ROWS, X * ROWS)
    straight = (shaped(X, 2, ROWS, W),) if part else (shaped(PARTS, 2, ROWS, W),) * X
    operands = (place, mark, own, other, *blocks[0], *blocks[1], *earlier)
    return call(functools.partial(product_kernel, part), (*straight, flipped, flipped), *operands)


def gate_kernel(*refs):
    refs[-1][...] = jnp.zeros_like(refs[-1])


def gate(*arrays):
    return pl.pallas_call(
        gate_kernel,
        out_shape=shaped(16, ROWS),
        in_specs=[VMEM] * len(arrays),
        out_specs=VMEM,
        cost_estimate=pl.CostEstimate(flops=10**12, bytes_accessed=0, transcendentals=0),
    )(*arrays)


def sum_kernel(place_ref, mark_ref, *refs):
    out_ref = refs[-1]
    here, zh, core = place_ref[0], place_ref[1], place_ref[2]
    for part in range(PARTS):
        for relative in range(C):
            number = lax.rem(core + relative, C)
            for dx in range(X):
                source = lax.rem(here + dx, X)
                to = source * WIDE + lax.rem(zh + part, ZH) * W + number * ROWS
                for pair in range(2):
                    straight = refs[-dx % X][part, pair, :, lanes(number * ROWS, ROWS)]
                    turned = refs[X + part * C + relative][pair, :, dx * ROWS : (dx + 1) * ROWS]
                    total = straight.astype(jnp.float32) + turned.astype(jnp.float32)
                    out_ref[pair, :, lanes(to, ROWS)] = total.astype(jnp.bfloat16)


def swap(array, axis, size, by):
    return lax.ppermute(array, axis, [(i, (i + by) % size) for i in range(size)])


def to_mirror(block, dz, dc):
    pairs = [
        ((y * ZH + z) * C + c, ((y + Y // 2) % Y * ZH + (z + dz) % ZH) * C + (c + dc) % C)
        for y in range(Y)
        for z in range(ZH)
        for c in range(C)
    ]
    return lax.ppermute(block, ("y", "zh", "c"), pairs)


def local(amplitudes, tile_mask, cycle_integral):
    place = jnp.stack([lax.axis_index(a) for a in ("x", "zh", "c")]).astype(jnp.int32)
    one = shaped(ROWS, NV)
    outs = (shaped(D, ROWS, WIDE), one, one)
    sent, *masked = call(first_kernel, outs, place, cycle_integral, amplitudes, tile_mask)
    own = lax.all_to_all(sent, ("x", "zh"), split_axis=0, concat_axis=0, tiled=True)

    right = [swap(m, "x", X, -1) for m in masked]
    left = [swap(m, "x", X, 1) for m in masked]
    across = [swap(right[0], "x", X, -1), swap(left[1], "x", X, 1)]
    blocks = [(masked[p], right[p], across[p], left[p]) for p in range(2)]
    other = swap(own, "c", C, 1)
    mark = gate(*across, right[1], left[0])

    later, same, cross = product(1, place, mark, own, other, blocks)
    outer = [to_mirror(same, 1, 0), to_mirror(cross, 1, 1)]
    *straight, same, cross = product(0, place, mark, own, other, blocks, later)
    inner = [to_mirror(same, 0, 0), to_mirror(cross, 0, 1)]
    straight = [swap(s, "x", X, dx) if dx else s for dx, s in enumerate(straight)]
    mark = gate(*inner, gate(*outer))
    return call(sum_kernel, shaped(2, ROWS, NV), place, mark, *straight, *inner, *outer)


def solution(mesh):
    split = Mesh(mesh.devices.reshape(Y, ZL, X, ZH, C), ("y", "zl", "x", "zh", "c"))
    pair, virt = ("y", "zl"), ("x", "zh", "c")
    return jax.shard_map(
        local,
        mesh=split,
        in_specs=(P(pair, virt, None), P(pair, virt, None), P(virt, None)),
        out_specs=P(pair, virt, None),
        check_vma=False,
    )
```

```python
import functools

import jax
import jax.numpy as jnp
from jax import lax
from jax.experimental import pallas as pl
from jax.experimental.pallas import tpu as pltpu
from jax.sharding import Mesh, PartitionSpec as P

TILE = 64
X, ZH, C, Y, ZL = 4, 2, 2, 8, 6
D = X * ZH
ROWS = 128
W = C * ROWS
NV = D * W
WIDE = ZH * W
PARTS = 2

VMEM = pl.BlockSpec(memory_space=pltpu.VMEM)
SMEM = pl.BlockSpec(memory_space=pltpu.SMEM)
LIMIT = 16 * 1024 * 1024


def call(kernel, out_shape, *operands, flops=0):
    many = isinstance(out_shape, tuple)
    first = SMEM if operands[0].ndim == 1 else VMEM
    return pl.pallas_call(
        kernel,
        out_shape=out_shape,
        in_specs=[first] + [VMEM] * (len(operands) - 1),
        out_specs=(VMEM,) * len(out_shape) if many else VMEM,
        compiler_params=pltpu.CompilerParams(vmem_limit_bytes=LIMIT),
        cost_estimate=pl.CostEstimate(flops=flops, bytes_accessed=0, transcendentals=0),
    )(*operands)


def shaped(*shape):
    return jax.ShapeDtypeStruct(shape, jnp.bfloat16)


def lanes(start, size):
    return pl.ds(pl.multiple_of(start, ROWS), size)


def first_kernel(x_ref, amp_ref, mask_ref, sent_ref, out_ref):
    for d in range(D):
        x = d // ZH
        for number in range(C):
            for z in range(ZH):
                at = (x * ZH + z) * W + number * ROWS
                sent_ref[d * C + number, :, z * ROWS : (z + 1) * ROWS] = x_ref[:, at : at + ROWS]
    blocks, tiles = mask_ref.shape[1:]
    spread = (
        lax.broadcasted_iota(jnp.int32, (tiles, NV), 1) // TILE
        == lax.broadcasted_iota(jnp.int32, (tiles, NV), 0)
    ).astype(jnp.bfloat16)
    for pair in range(2):
        rows = [
            jnp.broadcast_to(mask_ref[pair, b : b + 1, :].astype(jnp.float32), (TILE, tiles))
            for b in range(blocks)
        ]
        full = jnp.dot(
            jnp.concatenate(rows, axis=0).astype(jnp.bfloat16), spread, preferred_element_type=jnp.float32
        )
        out_ref[pair] = amp_ref[pair] * full.astype(jnp.bfloat16)


def product_kernel(place_ref, x_ref, *refs):
    blocks, (inner_ref, outer_ref, *straight_refs) = refs[:-4], refs[-4:]
    zh = place_ref[1]
    x = x_ref[...].reshape(NV, ZH * ROWS)
    for pair in range(2):
        rows = [r[pair] for r in blocks[:6]]
        rows[4:4] = [r[...] for r in blocks[6 + 2 * pair : 8 + 2 * pair]]
        found = jnp.dot(jnp.concatenate(rows, axis=0), x, preferred_element_type=jnp.float32)
        turned = found.T.astype(jnp.bfloat16)
        low, high = turned[:ROWS], turned[ROWS:]
        inner_ref[pair] = jnp.where(zh == 0, low, high)
        outer_ref[pair] = jnp.where(zh == 0, high, low)
        found = found.astype(jnp.bfloat16)
        for dx in range(X):
            for relative in range(C):
                at = (dx * C + relative) * ROWS
                straight_refs[relative][dx, pair] = found[at : at + ROWS]


def product(place, x, blocks):
    flipped, straight = shaped(2, ROWS, X * W), shaped(X, 2, ROWS, ZH * ROWS)
    return call(product_kernel, (flipped, flipped, straight, straight), place, x, *blocks)


def sum_kernel(place_ref, keep_ref, got_ref, *refs):
    out_ref = refs[-1]
    here, zh, core = place_ref[0], place_ref[1], place_ref[2]
    for part in range(PARTS):
        half = lax.rem(zh + part, ZH)
        for dx in range(X):
            for relative in range(C):
                x, number = lax.rem(here + dx, X), lax.rem(core + relative, C)
                at = (dx * C + relative) * ROWS
                to = (x * ZH + half) * W + number * ROWS
                source = refs[X - dx - 1].at[relative] if dx else (keep_ref, got_ref)[relative].at[0]
                for pair in range(2):
                    straight = source[pair, :, lanes(half * ROWS, ROWS)]
                    turned = refs[X - 1 + part][pair, :, at : at + ROWS]
                    total = straight.astype(jnp.float32) + turned.astype(jnp.float32)
                    out_ref[pair, :, lanes(to, ROWS)] = total.astype(jnp.bfloat16)


def swap(array, axis, size, by):
    return lax.ppermute(array, axis, [(i, (i + by) % size) for i in range(size)])


def to_mirror(block, dz):
    pairs = [
        (y * ZH + z, (y + Y // 2) % Y * ZH + (z + dz) % ZH) for y in range(Y) for z in range(ZH)
    ]
    return lax.ppermute(block, ("y", "zh"), pairs)


def local(amplitudes, tile_mask, cycle_integral):
    place = jnp.stack([lax.axis_index(a) for a in ("x", "zh", "c")]).astype(jnp.int32)
    outs = (shaped(D * C, ROWS, ZH * ROWS), shaped(2, ROWS, NV))
    sent, masked = call(first_kernel, outs, cycle_integral, amplitudes, tile_mask)

    right, left = swap(masked, "x", X, -1), swap(masked, "x", X, 1)
    across = [swap(right[0], "x", X, -1), swap(left[1], "x", X, 1)]
    blocks = []
    for block in (masked, right, left, *across):
        blocks += [block, swap(block, "c", C, 1)]
    x = lax.all_to_all(sent, ("x", "zh", "c"), split_axis=0, concat_axis=0, tiled=True)

    inner, outer, keep, give = product(place, x, blocks)
    inner, outer = to_mirror(inner, 0), to_mirror(outer, 1)
    got = swap(give, "c", C, 1)
    straight = [swap(jnp.stack([keep[dx], got[dx]]), "x", X, dx) for dx in range(1, X)]
    return call(sum_kernel, shaped(2, ROWS, NV), place, keep, got, *straight, inner, outer)


def solution(mesh):
    split = Mesh(mesh.devices.reshape(Y, ZL, X, ZH, C), ("y", "zl", "x", "zh", "c"))
    pair, virt = ("y", "zl"), ("x", "zh", "c")
    return jax.shard_map(
        local,
        mesh=split,
        in_specs=(P(pair, virt, None), P(pair, virt, None), P(virt, None)),
        out_specs=P(pair, virt, None),
        check_vma=False,
    )
```

```python
import functools

import jax
import jax.numpy as jnp
from jax import lax
from jax.experimental import pallas as pl
from jax.experimental.pallas import tpu as pltpu
from jax.sharding import Mesh, PartitionSpec as P

TILE = 64
X, ZH, C, Y, ZL = 4, 2, 2, 8, 6
D = X * ZH
ROWS = 128
W = C * ROWS
NV = D * W
N = D * ROWS
HALF = N // 2
STEP = 256

VMEM = pl.BlockSpec(memory_space=pltpu.VMEM)
SMEM = pl.BlockSpec(memory_space=pltpu.SMEM)
LIMIT = 16 * 1024 * 1024


def call(kernel, out_shape, *operands, flops=0):
    many = isinstance(out_shape, tuple)
    first = SMEM if operands[0].ndim == 1 else VMEM
    return pl.pallas_call(
        kernel,
        out_shape=out_shape,
        in_specs=[first] + [VMEM] * (len(operands) - 1),
        out_specs=(VMEM,) * len(out_shape) if many else VMEM,
        compiler_params=pltpu.CompilerParams(vmem_limit_bytes=LIMIT),
        cost_estimate=pl.CostEstimate(flops=flops, bytes_accessed=0, transcendentals=0),
    )(*operands)


def shaped(*shape):
    return jax.ShapeDtypeStruct(shape, jnp.bfloat16)


def lanes(start, size):
    return pl.ds(pl.multiple_of(start, ROWS), size)


def pick(core, x_ref, mine_ref, theirs_ref):
    for out_ref, number in ((mine_ref, core), (theirs_ref, 1 - core)):
        for d in range(D):
            half, at = divmod(d * ROWS, HALF)
            out_ref[half, :, at : at + ROWS] = x_ref[:, lanes(d * W + number * ROWS, ROWS)]


def first_kernel(place_ref, x_ref, amp_ref, mask_ref, mine_ref, theirs_ref, out_ref):
    pick(place_ref[1], x_ref, mine_ref, theirs_ref)
    zh, here = place_ref[0], place_ref[3]
    blocks, tiles = mask_ref.shape[1:]
    spread = (
        lax.broadcasted_iota(jnp.int32, (tiles, NV), 1) // TILE
        == lax.broadcasted_iota(jnp.int32, (tiles, NV), 0)
    ).astype(jnp.bfloat16)
    for pair in range(2):
        rows = [
            jnp.broadcast_to(mask_ref[pair, b : b + 1, :].astype(jnp.float32), (TILE, tiles))
            for b in range(blocks)
        ]
        full = jnp.dot(
            jnp.concatenate(rows, axis=0).astype(jnp.bfloat16), spread, preferred_element_type=jnp.float32
        )
        masked = amp_ref[pair] * full.astype(jnp.bfloat16)
        for d in range(D):
            x, z = divmod(d, ZH)
            to = jnp.where(zh == z, lax.rem(x + X - here, X) * W, x * W + NV // 2)
            out_ref[pair, :, lanes(to, W)] = masked[:, d * W : (d + 1) * W]


def chip_kernel(place_ref, mine_ref, got_ref, chip_ref, piece_ref):
    core, odd = place_ref[1], place_ref[2]
    for block_ref, number in ((mine_ref, core), (got_ref, 1 - core)):
        rows = lanes(number * ROWS, ROWS)
        chip_ref[:, rows, :] = block_ref[...]
        piece_ref[rows, :] = block_ref[odd]


def trade_kernel(place_ref, crossed_ref, traded_ref, *refs):
    spread_ref = refs[-1]
    odd = place_ref[2]
    for x in range(X):
        spread_ref[x, odd] = crossed_ref[...]
        spread_ref[x, 1 - odd] = traded_ref[...]


def rows_kernel(place_ref, mine_ref, theirs_ref, out_ref):
    for pair in range(2):
        out_ref[pair] = mine_ref[pair]
        out_ref[2 + pair] = theirs_ref[pair]


def products(rows, near_refs, far_ref):
    for column in range(0, N, STEP):
        half, at = divmod(column, HALF)
        blocks = [r[half, :, at : at + STEP] for r in near_refs] + [far_ref[x, half, :, at : at + STEP] for x in range(X)]
        x = jnp.concatenate(blocks, axis=0)
        yield column, jnp.dot(rows, x, preferred_element_type=jnp.float32)


def flip_kernel(place_ref, rows_ref, *refs):
    core, out_ref = place_ref[1], refs[-1]
    for column, found in products(rows_ref[...].reshape(2 * W, NV), refs[:X], refs[X]):
        turned = found.T.astype(jnp.bfloat16)
        for k in range(STEP // ROWS):
            block = turned[k * ROWS : (k + 1) * ROWS]
            for pair in range(2):
                for source in range(2):
                    start = (2 * source + pair) * ROWS
                    to = jnp.where(core == source, 0, ROWS)
                    out_ref[column // ROWS + k, pair, :, lanes(to, ROWS)] = block[:, start : start + ROWS]


def own_kernel(place_ref, mine_ref, theirs_ref, *refs):
    keep_ref, send_ref = refs[-2:]
    rows = jnp.concatenate([mine_ref[0], mine_ref[1], theirs_ref[0], theirs_ref[1]], axis=0)
    for column, found in products(rows, refs[:X], refs[X]):
        found = found.astype(jnp.bfloat16)
        for pair in range(2):
            keep_ref[pair, :, column : column + STEP] = found[pair * ROWS : (pair + 1) * ROWS]
            send_ref[pair, :, column : column + STEP] = found[(2 + pair) * ROWS : (3 + pair) * ROWS]


def sum_kernel(place_ref, keep_ref, got_ref, flips_ref, out_ref):
    core = place_ref[1]
    for d in range(D):
        for number, straight_ref in enumerate((keep_ref, got_ref)):
            at = jnp.where(core == number, 0, ROWS)
            for pair in range(2):
                turned = flips_ref[d, pair, :, lanes(at, ROWS)].astype(jnp.float32)
                straight = straight_ref[pair, :, d * ROWS : (d + 1) * ROWS].astype(jnp.float32)
                out_ref[pair, :, lanes(d * W + at, ROWS)] = (straight + turned).astype(jnp.bfloat16)


def swap(array, axis, size, by):
    return lax.ppermute(array, axis, [(i, (i + by) % size) for i in range(size)])


def over_x(spread):
    return lax.all_to_all(spread, "x", split_axis=0, concat_axis=0, tiled=True)


def local(amplitudes, tile_mask, cycle_integral):
    place = jnp.stack([lax.axis_index("zh"), lax.axis_index("c"), lax.axis_index("y") % 2, lax.axis_index("x")])
    place = place.astype(jnp.int32)
    half = shaped(2, ROWS, HALF)
    outs = (half, half, shaped(2, ROWS, NV))
    mine, theirs, masked = call(first_kernel, outs, place, cycle_integral, amplitudes, tile_mask)
    got = swap(theirs, "c", C, 1)
    mirrored = swap(masked, "y", Y, Y // 2)

    everywhere = shaped(X, 2, W, HALF)
    chip, piece = call(chip_kernel, (shaped(2, W, HALF), shaped(W, HALF)), place, mine, got)
    crossed = swap(piece, "zh", ZH, 1)
    traded = lax.ppermute(crossed, "y", [(i, i ^ 1) for i in range(Y)])
    near = [swap(chip, "x", X, -d) for d in range(1, X)]
    far = over_x(call(trade_kernel, everywhere, place, crossed, traded, *near, flops=0))
    near = [chip, *near]


    rows = call(rows_kernel, shaped(4, ROWS, NV), place, mirrored, swap(mirrored, "c", C, 1), flops=5000000000)
    masked_pair = swap(masked, "c", C, 1)
    out = call(flip_kernel, shaped(D, 2, ROWS, W), place, rows, *near, far)
    flips = lax.all_to_all(out, ("x", "zh"), split_axis=0, concat_axis=0, tiled=True)
    keep, send = call(own_kernel, (shaped(2, ROWS, N),) * 2, place, masked, masked_pair, *near, far)
    got = swap(send, "c", C, 1)
    return call(sum_kernel, shaped(2, ROWS, NV), place, keep, got, flips)


def solution(mesh):
    split = Mesh(mesh.devices.reshape(Y, ZL, X, ZH, C), ("y", "zl", "x", "zh", "c"))
    pair, virt = ("y", "zl"), ("x", "zh", "c")
    return jax.shard_map(
        local,
        mesh=split,
        in_specs=(P(pair, virt, None), P(pair, virt, None), P(virt, None)),
        out_specs=P(pair, virt, None),
        check_vma=False,
    )
```

```python
import functools

import jax
import jax.numpy as jnp
from jax import lax
from jax.experimental import pallas as pl
from jax.experimental.pallas import tpu as pltpu
from jax.sharding import Mesh, PartitionSpec as P

TILE = 64
X, ZH, C, Y, ZL = 4, 2, 2, 8, 6
D = X * ZH
ROWS = 128
W = C * ROWS
NV = D * W
N = D * ROWS
HALF = N // 2
STEP = 256

VMEM = pl.BlockSpec(memory_space=pltpu.VMEM)
SMEM = pl.BlockSpec(memory_space=pltpu.SMEM)
LIMIT = 16 * 1024 * 1024


def call(kernel, out_shape, *operands, flops=0):
    many = isinstance(out_shape, tuple)
    first = SMEM if operands[0].ndim == 1 else VMEM
    return pl.pallas_call(
        kernel,
        out_shape=out_shape,
        in_specs=[first] + [VMEM] * (len(operands) - 1),
        out_specs=(VMEM,) * len(out_shape) if many else VMEM,
        compiler_params=pltpu.CompilerParams(vmem_limit_bytes=LIMIT),
        cost_estimate=pl.CostEstimate(flops=flops, bytes_accessed=0, transcendentals=0),
    )(*operands)


def shaped(*shape):
    return jax.ShapeDtypeStruct(shape, jnp.bfloat16)


def lanes(start, size):
    return pl.ds(pl.multiple_of(start, ROWS), size)


def pick(core, x_ref, mine_ref, theirs_ref):
    for out_ref, number in ((mine_ref, core), (theirs_ref, 1 - core)):
        for d in range(D):
            half, at = divmod(d * ROWS, HALF)
            out_ref[half, :, at : at + ROWS] = x_ref[:, lanes(d * W + number * ROWS, ROWS)]


def first_kernel(place_ref, x_ref, amp_ref, mask_ref, mine_ref, theirs_ref, out_ref):
    pick(place_ref[1], x_ref, mine_ref, theirs_ref)
    zh, here = place_ref[0], place_ref[2]
    blocks, tiles = mask_ref.shape[1:]
    spread = (
        lax.broadcasted_iota(jnp.int32, (tiles, NV), 1) // TILE
        == lax.broadcasted_iota(jnp.int32, (tiles, NV), 0)
    ).astype(jnp.bfloat16)
    for pair in range(2):
        rows = [
            jnp.broadcast_to(mask_ref[pair, b : b + 1, :].astype(jnp.float32), (TILE, tiles))
            for b in range(blocks)
        ]
        full = jnp.dot(
            jnp.concatenate(rows, axis=0).astype(jnp.bfloat16), spread, preferred_element_type=jnp.float32
        )
        masked = amp_ref[pair] * full.astype(jnp.bfloat16)
        for d in range(D):
            x, z = divmod(d, ZH)
            to = jnp.where(zh == z, x * W, lax.rem(x + X - here, X) * W + NV // 2)
            out_ref[pair, :, lanes(to, W)] = masked[:, d * W : (d + 1) * W]


def chip_kernel(place_ref, mine_ref, got_ref, *part_refs):
    core = place_ref[1]
    for block_ref, number in ((mine_ref, core), (got_ref, 1 - core)):
        for half, part_ref in enumerate(part_refs):
            part_ref[lanes(number * ROWS, ROWS), :] = block_ref[half]


def far_kernel(*refs):
    for half in range(2):
        for dx in range(X):
            refs[-1][half, dx] = refs[half * X + dx][...]


def products(mine_ref, theirs_ref, near_refs, far_ref):
    rows = jnp.concatenate([mine_ref[0], mine_ref[1], theirs_ref[0], theirs_ref[1]], axis=0)
    for column in range(0, N, STEP):
        half, at = divmod(column, HALF)
        own = near_refs[half][:, :, at : at + STEP].reshape(NV // 2, STEP)
        other = far_ref[half, :, :, at : at + STEP].reshape(NV // 2, STEP)
        yield column, jnp.dot(rows, jnp.concatenate([own, other], axis=0), preferred_element_type=jnp.float32)


def flip_kernel(place_ref, mine_ref, theirs_ref, *refs):
    core, out_ref = place_ref[1], refs[-1]
    for column, found in products(mine_ref, theirs_ref, refs[:2], refs[2]):
        turned = found.T.astype(jnp.bfloat16)
        for k in range(STEP // ROWS):
            block = turned[k * ROWS : (k + 1) * ROWS]
            for pair in range(2):
                for source in range(2):
                    start = (2 * source + pair) * ROWS
                    to = jnp.where(core == source, 0, ROWS)
                    out_ref[column // ROWS + k, pair, :, lanes(to, ROWS)] = block[:, start : start + ROWS]


def own_kernel(place_ref, mine_ref, theirs_ref, *refs):
    keep_ref, send_ref = refs[-2:]
    for column, found in products(mine_ref, theirs_ref, refs[:2], refs[2]):
        found = found.astype(jnp.bfloat16)
        for pair in range(2):
            keep_ref[pair, :, column : column + STEP] = found[pair * ROWS : (pair + 1) * ROWS]
            send_ref[pair, :, column : column + STEP] = found[(2 + pair) * ROWS : (3 + pair) * ROWS]


def sum_kernel(place_ref, keep_ref, got_ref, flips_ref, out_ref):
    core = place_ref[1]
    for d in range(D):
        for number, straight_ref in enumerate((keep_ref, got_ref)):
            at = jnp.where(core == number, 0, ROWS)
            for pair in range(2):
                turned = flips_ref[d, pair, :, lanes(at, ROWS)].astype(jnp.float32)
                straight = straight_ref[pair, :, d * ROWS : (d + 1) * ROWS].astype(jnp.float32)
                out_ref[pair, :, lanes(d * W + at, ROWS)] = (straight + turned).astype(jnp.bfloat16)


def swap(array, axis, size, by):
    return lax.ppermute(array, axis, [(i, (i + by) % size) for i in range(size)])


def over_x(spread):
    return lax.all_to_all(spread, "x", split_axis=0, concat_axis=0, tiled=True)


def local(amplitudes, tile_mask, cycle_integral):
    place = jnp.stack([lax.axis_index("zh"), lax.axis_index("c"), lax.axis_index("x")])
    place = place.astype(jnp.int32)
    half = shaped(2, ROWS, HALF)
    outs = (half, half, shaped(2, ROWS, NV))
    mine, theirs, masked = call(first_kernel, outs, place, cycle_integral, amplitudes, tile_mask)
    got = swap(theirs, "c", C, 1)
    mirrored = swap(masked, "y", Y, Y // 2)

    parts = call(chip_kernel, (shaped(W, HALF),) * 2, place, mine, got)
    crossed = [swap(part, "zh", ZH, 1) for part in parts]
    near = [lax.all_gather(part, "x") for part in parts]
    far = []
    for block in crossed:
        far += [block] + [swap(block, "x", X, -d) for d in range(1, X)]

    far = call(far_kernel, shaped(2, X, W, HALF), *far, flops=10000000000)
    mirrored_pair = swap(mirrored, "c", C, 1)
    masked_pair = swap(masked, "c", C, 1)
    out = call(flip_kernel, shaped(D, 2, ROWS, W), place, mirrored, mirrored_pair, *near, far)
    flips = lax.all_to_all(out, ("x", "zh"), split_axis=0, concat_axis=0, tiled=True)
    keep, send = call(own_kernel, (shaped(2, ROWS, N),) * 2, place, masked, masked_pair, *near, far)
    got = swap(send, "c", C, 1)
    return call(sum_kernel, shaped(2, ROWS, NV), place, keep, got, flips)


def solution(mesh):
    split = Mesh(mesh.devices.reshape(Y, ZL, X, ZH, C), ("y", "zl", "x", "zh", "c"))
    pair, virt = ("y", "zl"), ("x", "zh", "c")
    return jax.shard_map(
        local,
        mesh=split,
        in_specs=(P(pair, virt, None), P(pair, virt, None), P(virt, None)),
        out_specs=P(pair, virt, None),
        check_vma=False,
    )
```

```python
import functools

import jax
import jax.numpy as jnp
from jax import lax
from jax.experimental import pallas as pl
from jax.experimental.pallas import tpu as pltpu
from jax.sharding import Mesh, PartitionSpec as P

TILE = 64
X, ZH, C, Y, ZL = 4, 2, 2, 8, 6
D = X * ZH
ROWS = 128
W = C * ROWS
NV = D * W
WIDE = ZH * W
CUTS = 2
PARTS = 2

VMEM = pl.BlockSpec(memory_space=pltpu.VMEM)
SMEM = pl.BlockSpec(memory_space=pltpu.SMEM)
LIMIT = 16 * 1024 * 1024


def call(kernel, out_shape, *operands, flops=0):
    many = isinstance(out_shape, tuple)
    first = SMEM if operands[0].ndim == 1 else VMEM
    return pl.pallas_call(
        kernel,
        out_shape=out_shape,
        in_specs=[first] + [VMEM] * (len(operands) - 1),
        out_specs=(VMEM,) * len(out_shape) if many else VMEM,
        compiler_params=pltpu.CompilerParams(vmem_limit_bytes=LIMIT),
        cost_estimate=pl.CostEstimate(flops=flops, bytes_accessed=0, transcendentals=0),
    )(*operands)


def shaped(*shape):
    return jax.ShapeDtypeStruct(shape, jnp.bfloat16)


def lanes(start, size):
    return pl.ds(pl.multiple_of(start, ROWS), size)


def first_kernel(x_ref, amp_ref, mask_ref, sent_ref, out_ref):
    for d in range(D):
        x = d // ZH
        for number in range(C):
            for z in range(ZH):
                at = (x * ZH + z) * W + number * ROWS
                sent_ref[d * C + number, :, z * ROWS : (z + 1) * ROWS] = x_ref[:, at : at + ROWS]
    blocks, tiles = mask_ref.shape[1:]
    spread = (
        lax.broadcasted_iota(jnp.int32, (tiles, NV), 1) // TILE
        == lax.broadcasted_iota(jnp.int32, (tiles, NV), 0)
    ).astype(jnp.bfloat16)
    for pair in range(2):
        rows = [
            jnp.broadcast_to(mask_ref[pair, b : b + 1, :].astype(jnp.float32), (TILE, tiles))
            for b in range(blocks)
        ]
        full = jnp.dot(
            jnp.concatenate(rows, axis=0).astype(jnp.bfloat16), spread, preferred_element_type=jnp.float32
        )
        out_ref[pair] = amp_ref[pair] * full.astype(jnp.bfloat16)


def halves_kernel(right_ref, left_ref, from_right_ref, from_left_ref):
    from_right_ref[...] = right_ref[0]
    from_left_ref[...] = left_ref[1]


def product_kernel(place_ref, x_ref, *refs):
    blocks, inner_ref, outer_refs, straight_ref = refs[:10], refs[10], refs[11:-1], refs[-1]
    here, zh, core = place_ref[0], place_ref[1], place_ref[2]
    x = x_ref[...].reshape(NV, ZH * ROWS)
    for pair in range(2):
        rows = [r[pair] for r in blocks[:6]]
        rows[4:4] = [r[...] for r in blocks[6 + 2 * pair : 8 + 2 * pair]]
        found = jnp.dot(jnp.concatenate(rows, axis=0), x, preferred_element_type=jnp.float32)
        turned = found.T.astype(jnp.bfloat16)
        low, high = turned[:ROWS], turned[ROWS:]
        inner_ref[pair] = jnp.where(zh == 0, low, high)
        outer = jnp.where(zh == 0, high, low)
        for cut in range(CUTS):
            outer_refs[pair * CUTS + cut][...] = outer[:, cut * X * W // CUTS : (cut + 1) * X * W // CUTS]
        found = found.astype(jnp.bfloat16)
        for dx in range(X):
            for relative in range(C):
                to = lax.rem(here + dx, X) * C + lax.rem(core + relative, C)
                at = (dx * C + relative) * ROWS
                straight_ref[to, pair] = found[at : at + ROWS]


def product(place, x, blocks):
    outs = (shaped(2, ROWS, X * W),) + (shaped(ROWS, X * W // CUTS),) * (2 * CUTS) + (shaped(X * C, 2, ROWS, ZH * ROWS),)
    inner, *outer, straight = call(product_kernel, outs, place, x, *blocks)
    return inner, outer, straight


def flips_kernel(inner_ref, *refs):
    out_ref = refs[-1]
    out_ref[0] = inner_ref[...]
    for pair in range(2):
        for cut in range(CUTS):
            out_ref[1, pair, :, cut * X * W // CUTS : (cut + 1) * X * W // CUTS] = refs[pair * CUTS + cut][...]


def sum_kernel(place_ref, straight_ref, flips_ref, out_ref):
    here, zh, core = place_ref[0], place_ref[1], place_ref[2]
    for part in range(PARTS):
        half = lax.rem(zh + part, ZH)
        for dx in range(X):
            for relative in range(C):
                x, number = lax.rem(here + dx, X), lax.rem(core + relative, C)
                at = (dx * C + relative) * ROWS
                to = (x * ZH + half) * W + number * ROWS
                for pair in range(2):
                    straight = straight_ref[x * C + number, pair, :, lanes(half * ROWS, ROWS)]
                    turned = flips_ref[part, pair, :, at : at + ROWS]
                    total = straight.astype(jnp.float32) + turned.astype(jnp.float32)
                    out_ref[pair, :, lanes(to, ROWS)] = total.astype(jnp.bfloat16)


def swap(array, axis, size, by):
    return lax.ppermute(array, axis, [(i, (i + by) % size) for i in range(size)])


def to_mirror(block, dz):
    pairs = [
        (y * ZH + z, (y + Y // 2) % Y * ZH + (z + dz) % ZH) for y in range(Y) for z in range(ZH)
    ]
    return lax.ppermute(block, ("y", "zh"), pairs)


def local(amplitudes, tile_mask, cycle_integral):
    place = jnp.stack([lax.axis_index(a) for a in ("x", "zh", "c")]).astype(jnp.int32)
    outs = (shaped(D * C, ROWS, ZH * ROWS), shaped(2, ROWS, NV))
    sent, masked = call(first_kernel, outs, cycle_integral, amplitudes, tile_mask)

    right, left = swap(masked, "x", X, -1), swap(masked, "x", X, 1)
    one = shaped(ROWS, NV)
    from_right, from_left = call(halves_kernel, (one, one), right, left, flops=12000000000)
    across = [swap(from_right, "x", X, -1), swap(from_left, "x", X, 1)]
    blocks = []
    for block in (masked, right, left, *across):
        blocks += [block, swap(block, "c", C, 1)]
    x = lax.all_to_all(sent, ("x", "zh", "c"), split_axis=0, concat_axis=0, tiled=True)

    inner, outer, straight = product(place, x, blocks)
    inner, outer = to_mirror(inner, 0), [to_mirror(block, 1) for block in outer]
    straight = lax.all_to_all(straight, ("x", "c"), split_axis=0, concat_axis=0, tiled=True)
    flips = call(flips_kernel, shaped(PARTS, 2, ROWS, X * W), inner, *outer, flops=10**11)
    return call(sum_kernel, shaped(2, ROWS, NV), place, straight, flips)


def solution(mesh):
    split = Mesh(mesh.devices.reshape(Y, ZL, X, ZH, C), ("y", "zl", "x", "zh", "c"))
    pair, virt = ("y", "zl"), ("x", "zh", "c")
    return jax.shard_map(
        local,
        mesh=split,
        in_specs=(P(pair, virt, None), P(pair, virt, None), P(virt, None)),
        out_specs=P(pair, virt, None),
        check_vma=False,
    )
```

```python
import functools

import jax
import jax.numpy as jnp
from jax import lax
from jax.experimental import pallas as pl
from jax.experimental.pallas import tpu as pltpu
from jax.sharding import Mesh, PartitionSpec as P

TILE = 64
X, ZH, C, Y, ZL = 4, 2, 2, 8, 6
D = X * ZH
ROWS = 128
W = C * ROWS
NV = D * W
WIDE = ZH * W
PARTS = 2

VMEM = pl.BlockSpec(memory_space=pltpu.VMEM)
SMEM = pl.BlockSpec(memory_space=pltpu.SMEM)
LIMIT = 16 * 1024 * 1024


def call(kernel, out_shape, *operands, flops=0):
    many = isinstance(out_shape, tuple)
    first = SMEM if operands[0].ndim == 1 else VMEM
    return pl.pallas_call(
        kernel,
        out_shape=out_shape,
        in_specs=[first] + [VMEM] * (len(operands) - 1),
        out_specs=(VMEM,) * len(out_shape) if many else VMEM,
        compiler_params=pltpu.CompilerParams(vmem_limit_bytes=LIMIT),
        cost_estimate=pl.CostEstimate(flops=flops, bytes_accessed=0, transcendentals=0),
    )(*operands)


def shaped(*shape):
    return jax.ShapeDtypeStruct(shape, jnp.bfloat16)


def lanes(start, size):
    return pl.ds(pl.multiple_of(start, ROWS), size)


def first_kernel(x_ref, amp_ref, mask_ref, sent_ref, out_ref):
    for d in range(D):
        x = d // ZH
        for number in range(C):
            for z in range(ZH):
                at = (x * ZH + z) * W + number * ROWS
                sent_ref[d * C + number, :, z * ROWS : (z + 1) * ROWS] = x_ref[:, at : at + ROWS]
    blocks, tiles = mask_ref.shape[1:]
    spread = (
        lax.broadcasted_iota(jnp.int32, (tiles, NV), 1) // TILE
        == lax.broadcasted_iota(jnp.int32, (tiles, NV), 0)
    ).astype(jnp.bfloat16)
    for pair in range(2):
        rows = [
            jnp.broadcast_to(mask_ref[pair, b : b + 1, :].astype(jnp.float32), (TILE, tiles))
            for b in range(blocks)
        ]
        full = jnp.dot(
            jnp.concatenate(rows, axis=0).astype(jnp.bfloat16), spread, preferred_element_type=jnp.float32
        )
        out_ref[pair] = amp_ref[pair] * full.astype(jnp.bfloat16)


def halves_kernel(right_ref, left_ref, from_right_ref, from_left_ref):
    from_right_ref[...] = right_ref[0]
    from_left_ref[...] = left_ref[1]


def product_kernel(place_ref, x_ref, *refs):
    blocks, (inner_ref, outer_ref, straight_ref) = refs[:-3], refs[-3:]
    here, zh, core = place_ref[0], place_ref[1], place_ref[2]
    x = x_ref[...].reshape(NV, ZH * ROWS)
    for pair in range(2):
        rows = [r[pair] for r in blocks[:6]]
        rows[4:4] = [r[...] for r in blocks[6 + 2 * pair : 8 + 2 * pair]]
        found = jnp.dot(jnp.concatenate(rows, axis=0), x, preferred_element_type=jnp.float32)
        turned = found.T.astype(jnp.bfloat16)
        low, high = turned[:ROWS], turned[ROWS:]
        inner_ref[pair] = jnp.where(zh == 0, low, high)
        outer_ref[pair] = jnp.where(zh == 0, high, low)
        found = found.astype(jnp.bfloat16)
        for dx in range(X):
            for relative in range(C):
                to = lax.rem(here + dx, X) * C + lax.rem(core + relative, C)
                at = (dx * C + relative) * ROWS
                straight_ref[to, pair] = found[at : at + ROWS]


def product(place, x, blocks):
    flipped = shaped(2, ROWS, X * W)
    return call(product_kernel, (flipped, flipped, shaped(X * C, 2, ROWS, ZH * ROWS)), place, x, *blocks)


def sum_kernel(place_ref, straight_ref, *refs):
    out_ref = refs[-1]
    here, zh, core = place_ref[0], place_ref[1], place_ref[2]
    for part in range(PARTS):
        half = lax.rem(zh + part, ZH)
        for dx in range(X):
            for relative in range(C):
                x, number = lax.rem(here + dx, X), lax.rem(core + relative, C)
                at = (dx * C + relative) * ROWS
                to = (x * ZH + half) * W + number * ROWS
                for pair in range(2):
                    straight = straight_ref[x * C + number, pair, :, lanes(half * ROWS, ROWS)]
                    turned = refs[part][pair, :, at : at + ROWS]
                    total = straight.astype(jnp.float32) + turned.astype(jnp.float32)
                    out_ref[pair, :, lanes(to, ROWS)] = total.astype(jnp.bfloat16)


def swap(array, axis, size, by):
    return lax.ppermute(array, axis, [(i, (i + by) % size) for i in range(size)])


def half_way(block):
    def place(y, z, x_c):
        return (y % Y * ZL + z % (ZH * ZL) % ZL) * ZH * C + z % (ZH * ZL) // ZL * C + x_c

    pairs = []
    for y in range(Y):
        for z in range(ZH * ZL):
            for c, way in ((0, 1), (1, -1)):
                pairs.append((place(y, z, c), place(y + way * Y // 4, z + way * ZH * ZL // 4, c)))
    return lax.ppermute(block, ("y", "zl", "zh", "c"), pairs)


def local(amplitudes, tile_mask, cycle_integral):
    place = jnp.stack([lax.axis_index(a) for a in ("x", "zh", "c")]).astype(jnp.int32)
    outs = (shaped(D * C, ROWS, ZH * ROWS), shaped(2, ROWS, NV))
    sent, masked = call(first_kernel, outs, cycle_integral, amplitudes, tile_mask)

    right, left = swap(masked, "x", X, -1), swap(masked, "x", X, 1)
    one = shaped(ROWS, NV)
    from_right, from_left = call(halves_kernel, (one, one), right, left, flops=12 * 10**9)
    across = [swap(from_right, "x", X, -1), swap(from_left, "x", X, 1)]
    blocks = []
    for block in (masked, right, left, *across):
        blocks += [block, swap(block, "c", C, 1)]
    x = lax.all_to_all(sent, ("x", "zh", "c"), split_axis=0, concat_axis=0, tiled=True)

    inner, outer, straight = product(place, x, blocks)
    inner, outer = swap(inner, "y", Y, Y // 2), half_way(half_way(outer))
    straight = lax.all_to_all(straight, ("x", "c"), split_axis=0, concat_axis=0, tiled=True)
    return call(sum_kernel, shaped(2, ROWS, NV), place, straight, inner, outer)


def solution(mesh):
    split = Mesh(mesh.devices.reshape(Y, ZL, X, ZH, C), ("y", "zl", "x", "zh", "c"))
    pair, virt = ("y", "zl"), ("x", "zh", "c")
    return jax.shard_map(
        local,
        mesh=split,
        in_specs=(P(pair, virt, None), P(pair, virt, None), P(virt, None)),
        out_specs=P(pair, virt, None),
        check_vma=False,
    )
```

```python
import functools

import jax
import jax.numpy as jnp
from jax import lax
from jax.experimental import pallas as pl
from jax.experimental.pallas import tpu as pltpu
from jax.sharding import Mesh, PartitionSpec as P

TILE = 64
X, ZH, C, Y, ZL = 4, 2, 2, 8, 6
D = X * ZH
ROWS = 128
W = C * ROWS
NV = D * W
N = D * ROWS
STEP = 256

VMEM = pl.BlockSpec(memory_space=pltpu.VMEM)
SMEM = pl.BlockSpec(memory_space=pltpu.SMEM)
LIMIT = 16 * 1024 * 1024


def call(kernel, out_shape, *operands, flops=0):
    many = isinstance(out_shape, tuple)
    first = SMEM if operands[0].ndim == 1 else VMEM
    return pl.pallas_call(
        kernel,
        out_shape=out_shape,
        in_specs=[first] + [VMEM] * (len(operands) - 1),
        out_specs=(VMEM,) * len(out_shape) if many else VMEM,
        compiler_params=pltpu.CompilerParams(vmem_limit_bytes=LIMIT),
        cost_estimate=pl.CostEstimate(flops=flops, bytes_accessed=0, transcendentals=0),
    )(*operands)


def shaped(*shape):
    return jax.ShapeDtypeStruct(shape, jnp.bfloat16)


def lanes(start, size):
    return pl.ds(pl.multiple_of(start, ROWS), size)


def pick_kernel(place_ref, x_ref, mine_ref, theirs_ref):
    core = place_ref[1]
    for out_ref, number in ((mine_ref, core), (theirs_ref, 1 - core)):
        for d in range(D):
            out_ref[:, d * ROWS : (d + 1) * ROWS] = x_ref[:, lanes(d * W + number * ROWS, ROWS)]


def mask_kernel(place_ref, amp_ref, mask_ref, out_ref):
    zh, here = place_ref[0], place_ref[2]
    blocks, tiles = mask_ref.shape[1:]
    spread = (
        lax.broadcasted_iota(jnp.int32, (tiles, NV), 1) // TILE
        == lax.broadcasted_iota(jnp.int32, (tiles, NV), 0)
    ).astype(jnp.bfloat16)
    for pair in range(2):
        rows = [
            jnp.broadcast_to(mask_ref[pair, b : b + 1, :].astype(jnp.float32), (TILE, tiles))
            for b in range(blocks)
        ]
        full = jnp.dot(
            jnp.concatenate(rows, axis=0).astype(jnp.bfloat16), spread, preferred_element_type=jnp.float32
        )
        masked = amp_ref[pair] * full.astype(jnp.bfloat16)
        for d in range(D):
            x, z = divmod(d, ZH)
            to = lax.rem(x + X - here, X) * W + jnp.where(zh == z, 0, NV // 2)
            out_ref[pair, :, lanes(to, W)] = masked[:, d * W : (d + 1) * W]


def chip_kernel(place_ref, mine_ref, got_ref, chip_ref):
    core = place_ref[1]
    chip_ref[lanes(core * ROWS, ROWS), :] = mine_ref[...]
    chip_ref[lanes((1 - core) * ROWS, ROWS), :] = got_ref[...]


def copy_kernel(block_ref, *refs):
    refs[-1][...] = block_ref[...]


def far_kernel(*refs):
    for dx in range(X):
        refs[-1][dx] = refs[dx][...]


def products(mine_ref, theirs_ref, refs):
    rows = jnp.concatenate([mine_ref[0], mine_ref[1], theirs_ref[0], theirs_ref[1]], axis=0)
    for at in range(0, N, STEP):
        blocks = [r[:, at : at + STEP] for r in refs[:X]] + [refs[X][dx, :, at : at + STEP] for dx in range(X)]
        yield at, jnp.dot(rows, jnp.concatenate(blocks, axis=0), preferred_element_type=jnp.float32)


def flip_kernel(place_ref, mine_ref, theirs_ref, *refs):
    core, out_ref = place_ref[1], refs[-1]
    for column, found in products(mine_ref, theirs_ref, refs):
        turned = found.T.astype(jnp.bfloat16)
        for k in range(STEP // ROWS):
            block = turned[k * ROWS : (k + 1) * ROWS]
            for pair in range(2):
                for source in range(2):
                    start = (2 * source + pair) * ROWS
                    to = jnp.where(core == source, 0, ROWS)
                    out_ref[column // ROWS + k, pair, :, lanes(to, ROWS)] = block[:, start : start + ROWS]


def own_kernel(place_ref, mine_ref, theirs_ref, *refs):
    keep_ref, send_ref = refs[-2:]
    for column, found in products(mine_ref, theirs_ref, refs):
        found = found.astype(jnp.bfloat16)
        for pair in range(2):
            keep_ref[pair, :, column : column + STEP] = found[pair * ROWS : (pair + 1) * ROWS]
            send_ref[pair, :, column : column + STEP] = found[(2 + pair) * ROWS : (3 + pair) * ROWS]


def sum_kernel(place_ref, keep_ref, got_ref, flips_ref, out_ref):
    core = place_ref[1]
    for d in range(D):
        for number, straight_ref in enumerate((keep_ref, got_ref)):
            at = jnp.where(core == number, 0, ROWS)
            for pair in range(2):
                turned = flips_ref[d, pair, :, lanes(at, ROWS)].astype(jnp.float32)
                straight = straight_ref[pair, :, d * ROWS : (d + 1) * ROWS].astype(jnp.float32)
                out_ref[pair, :, lanes(d * W + at, ROWS)] = (straight + turned).astype(jnp.bfloat16)


def swap(array, axis, size, by):
    return lax.ppermute(array, axis, [(i, (i + by) % size) for i in range(size)])


def over_x(spread):
    return lax.all_to_all(spread, "x", split_axis=0, concat_axis=0, tiled=True)


def local(amplitudes, tile_mask, cycle_integral):
    place = jnp.stack([lax.axis_index("zh"), lax.axis_index("c"), lax.axis_index("x")])
    place = place.astype(jnp.int32)
    mine, theirs = call(pick_kernel, (shaped(ROWS, N),) * 2, place, cycle_integral)
    masked = call(mask_kernel, shaped(2, ROWS, NV), place, amplitudes, tile_mask)
    got = swap(theirs, "c", C, 1)
    mirrored = swap(masked, "y", Y, Y // 2)

    chip = call(chip_kernel, shaped(W, N), place, mine, got)
    near = [chip] + [swap(chip, "x", X, -d) for d in range(1, X)]
    crossed = swap(chip, "zh", ZH, 1)
    crossed = call(copy_kernel, shaped(W, N), crossed, flops=3 * 10**9)
    crossed = call(copy_kernel, shaped(W, N), crossed, *near[1:], flops=0)
    far = [crossed] + [swap(crossed, "x", X, -d) for d in range(1, X)]
    far = call(far_kernel, shaped(X, W, N), *far, flops=10**10)
    mirrored_pair = swap(mirrored, "c", C, 1)
    masked_pair = swap(masked, "c", C, 1)
    out = call(flip_kernel, shaped(D, 2, ROWS, W), place, mirrored, mirrored_pair, *near, far)
    flips = lax.all_to_all(out, ("x", "zh"), split_axis=0, concat_axis=0, tiled=True)
    keep, send = call(own_kernel, (shaped(2, ROWS, N),) * 2, place, masked, masked_pair, *near, far)
    got = swap(send, "c", C, 1)
    return call(sum_kernel, shaped(2, ROWS, NV), place, keep, got, flips)


def solution(mesh):
    split = Mesh(mesh.devices.reshape(Y, ZL, X, ZH, C), ("y", "zl", "x", "zh", "c"))
    pair, virt = ("y", "zl"), ("x", "zh", "c")
    return jax.shard_map(
        local,
        mesh=split,
        in_specs=(P(pair, virt, None), P(pair, virt, None), P(virt, None)),
        out_specs=P(pair, virt, None),
        check_vma=False,
    )
```

```python
import functools

import jax
import jax.numpy as jnp
from jax import lax
from jax.experimental import pallas as pl
from jax.experimental.pallas import tpu as pltpu
from jax.sharding import Mesh, PartitionSpec as P

TILE = 64
X, ZH, C, Y, ZL = 4, 2, 2, 8, 6
D = X * ZH
ROWS = 128
W = C * ROWS
NV = D * W
N = D * ROWS
STEP = 256

VMEM = pl.BlockSpec(memory_space=pltpu.VMEM)
SMEM = pl.BlockSpec(memory_space=pltpu.SMEM)
LIMIT = 16 * 1024 * 1024


def call(kernel, out_shape, *operands, flops=0):
    many = isinstance(out_shape, tuple)
    first = SMEM if operands[0].ndim == 1 else VMEM
    return pl.pallas_call(
        kernel,
        out_shape=out_shape,
        in_specs=[first] + [VMEM] * (len(operands) - 1),
        out_specs=(VMEM,) * len(out_shape) if many else VMEM,
        compiler_params=pltpu.CompilerParams(vmem_limit_bytes=LIMIT),
        cost_estimate=pl.CostEstimate(flops=flops, bytes_accessed=0, transcendentals=0),
    )(*operands)


def shaped(*shape):
    return jax.ShapeDtypeStruct(shape, jnp.bfloat16)


def lanes(start, size):
    return pl.ds(pl.multiple_of(start, ROWS), size)


def pick_kernel(place_ref, x_ref, mine_ref, theirs_ref):
    core = place_ref[1]
    for out_ref, number in ((mine_ref, core), (theirs_ref, 1 - core)):
        for d in range(D):
            out_ref[:, d * ROWS : (d + 1) * ROWS] = x_ref[:, lanes(d * W + number * ROWS, ROWS)]


def mask_kernel(place_ref, amp_ref, mask_ref, out_ref):
    zh, here = place_ref[0], place_ref[2]
    blocks, tiles = mask_ref.shape[1:]
    spread = (
        lax.broadcasted_iota(jnp.int32, (tiles, NV), 1) // TILE
        == lax.broadcasted_iota(jnp.int32, (tiles, NV), 0)
    ).astype(jnp.bfloat16)
    for pair in range(2):
        rows = [
            jnp.broadcast_to(mask_ref[pair, b : b + 1, :].astype(jnp.float32), (TILE, tiles))
            for b in range(blocks)
        ]
        full = jnp.dot(
            jnp.concatenate(rows, axis=0).astype(jnp.bfloat16), spread, preferred_element_type=jnp.float32
        )
        masked = amp_ref[pair] * full.astype(jnp.bfloat16)
        for d in range(D):
            x, z = divmod(d, ZH)
            to = lax.rem(x + X - here, X) * W + jnp.where(zh == z, 0, NV // 2)
            out_ref[pair, :, lanes(to, W)] = masked[:, d * W : (d + 1) * W]


def chip_kernel(place_ref, mine_ref, got_ref, chip_ref):
    core = place_ref[1]
    chip_ref[lanes(core * ROWS, ROWS), :] = mine_ref[...]
    chip_ref[lanes((1 - core) * ROWS, ROWS), :] = got_ref[...]


def copy_kernel(block_ref, *refs):
    refs[-1][...] = block_ref[...]


def far_kernel(*refs):
    for dx in range(X):
        refs[-1][dx] = refs[dx][...]


def products(mine_ref, theirs_ref, refs):
    rows = jnp.concatenate([mine_ref[0], mine_ref[1], theirs_ref[0], theirs_ref[1]], axis=0)
    for at in range(0, N, STEP):
        blocks = [r[:, at : at + STEP] for r in refs[:X]] + [refs[X][dx, :, at : at + STEP] for dx in range(X)]
        yield at, jnp.dot(rows, jnp.concatenate(blocks, axis=0), preferred_element_type=jnp.float32)


def flip_kernel(place_ref, mine_ref, theirs_ref, *refs):
    core, out_ref = place_ref[1], refs[-1]
    for column, found in products(mine_ref, theirs_ref, refs):
        turned = found.T.astype(jnp.bfloat16)
        for k in range(STEP // ROWS):
            block = turned[k * ROWS : (k + 1) * ROWS]
            for pair in range(2):
                for source in range(2):
                    start = (2 * source + pair) * ROWS
                    to = jnp.where(core == source, 0, ROWS)
                    out_ref[column // ROWS + k, pair, :, lanes(to, ROWS)] = block[:, start : start + ROWS]


def own_kernel(place_ref, mine_ref, theirs_ref, *refs):
    keep_ref, send_ref = refs[-2:]
    for column, found in products(mine_ref, theirs_ref, refs):
        found = found.astype(jnp.bfloat16)
        for pair in range(2):
            keep_ref[pair, :, column : column + STEP] = found[pair * ROWS : (pair + 1) * ROWS]
            send_ref[pair, :, column : column + STEP] = found[(2 + pair) * ROWS : (3 + pair) * ROWS]


def sum_kernel(place_ref, keep_ref, got_ref, flips_ref, out_ref):
    core = place_ref[1]
    for d in range(D):
        for number, straight_ref in enumerate((keep_ref, got_ref)):
            at = jnp.where(core == number, 0, ROWS)
            for pair in range(2):
                turned = flips_ref[d, pair, :, lanes(at, ROWS)].astype(jnp.float32)
                straight = straight_ref[pair, :, d * ROWS : (d + 1) * ROWS].astype(jnp.float32)
                out_ref[pair, :, lanes(d * W + at, ROWS)] = (straight + turned).astype(jnp.bfloat16)


def swap(array, axis, size, by):
    return lax.ppermute(array, axis, [(i, (i + by) % size) for i in range(size)])


def over_x(spread):
    return lax.all_to_all(spread, "x", split_axis=0, concat_axis=0, tiled=True)


def local(amplitudes, tile_mask, cycle_integral):
    place = jnp.stack([lax.axis_index("zh"), lax.axis_index("c"), lax.axis_index("x")])
    place = place.astype(jnp.int32)
    mine, theirs = call(pick_kernel, (shaped(ROWS, N),) * 2, place, cycle_integral)
    masked = call(mask_kernel, shaped(2, ROWS, NV), place, amplitudes, tile_mask)
    got = swap(theirs, "c", C, 1)
    mirrored = swap(masked, "y", Y, Y // 2)

    chip = call(chip_kernel, shaped(W, N), place, mine, got)
    near = [chip] + [swap(chip, "x", X, -d) for d in range(1, X)]
    crossed = swap(chip, "zh", ZH, 1)
    crossed = call(copy_kernel, shaped(W, N), crossed, flops=3 * 10**9)
    crossed = call(copy_kernel, shaped(W, N), crossed, *near[1:], flops=3 * 10**9)
    far = [crossed] + [swap(crossed, "x", X, -d) for d in range(1, X)]
    far = call(far_kernel, shaped(X, W, N), *far, flops=10**10)
    mirrored_pair = swap(mirrored, "c", C, 1)
    masked_pair = swap(masked, "c", C, 1)
    out = call(flip_kernel, shaped(D, 2, ROWS, W), place, mirrored, mirrored_pair, *near, far)
    flips = lax.all_to_all(out, ("x", "zh"), split_axis=0, concat_axis=0, tiled=True)
    keep, send = call(own_kernel, (shaped(2, ROWS, N),) * 2, place, masked, masked_pair, *near, far)
    got = swap(send, "c", C, 1)
    return call(sum_kernel, shaped(2, ROWS, NV), place, keep, got, flips)


def solution(mesh):
    split = Mesh(mesh.devices.reshape(Y, ZL, X, ZH, C), ("y", "zl", "x", "zh", "c"))
    pair, virt = ("y", "zl"), ("x", "zh", "c")
    return jax.shard_map(
        local,
        mesh=split,
        in_specs=(P(pair, virt, None), P(pair, virt, None), P(virt, None)),
        out_specs=P(pair, virt, None),
        check_vma=False,
    )
```

```python
import functools

import jax
import jax.numpy as jnp
from jax import lax
from jax.experimental import pallas as pl
from jax.experimental.pallas import tpu as pltpu
from jax.sharding import Mesh, PartitionSpec as P

TILE = 64
X, ZH, C, Y, ZL = 4, 2, 2, 8, 6
D = X * ZH
ROWS = 128
W = C * ROWS
NV = D * W
N = D * ROWS
STEP = 256

VMEM = pl.BlockSpec(memory_space=pltpu.VMEM)
SMEM = pl.BlockSpec(memory_space=pltpu.SMEM)
LIMIT = 16 * 1024 * 1024


def call(kernel, out_shape, *operands, flops=0):
    many = isinstance(out_shape, tuple)
    first = SMEM if operands[0].ndim == 1 else VMEM
    return pl.pallas_call(
        kernel,
        out_shape=out_shape,
        in_specs=[first] + [VMEM] * (len(operands) - 1),
        out_specs=(VMEM,) * len(out_shape) if many else VMEM,
        compiler_params=pltpu.CompilerParams(vmem_limit_bytes=LIMIT),
        cost_estimate=pl.CostEstimate(flops=flops, bytes_accessed=0, transcendentals=0),
    )(*operands)


def shaped(*shape):
    return jax.ShapeDtypeStruct(shape, jnp.bfloat16)


def lanes(start, size):
    return pl.ds(pl.multiple_of(start, ROWS), size)


def pick_kernel(place_ref, x_ref, mine_ref, theirs_ref):
    core = place_ref[1]
    for out_ref, number in ((mine_ref, core), (theirs_ref, 1 - core)):
        for d in range(D):
            out_ref[:, d * ROWS : (d + 1) * ROWS] = x_ref[:, lanes(d * W + number * ROWS, ROWS)]


def mask_kernel(place_ref, amp_ref, mask_ref, out_ref):
    zh, here = place_ref[0], place_ref[2]
    blocks, tiles = mask_ref.shape[1:]
    spread = (
        lax.broadcasted_iota(jnp.int32, (tiles, NV), 1) // TILE
        == lax.broadcasted_iota(jnp.int32, (tiles, NV), 0)
    ).astype(jnp.bfloat16)
    for pair in range(2):
        rows = [
            jnp.broadcast_to(mask_ref[pair, b : b + 1, :].astype(jnp.float32), (TILE, tiles))
            for b in range(blocks)
        ]
        full = jnp.dot(
            jnp.concatenate(rows, axis=0).astype(jnp.bfloat16), spread, preferred_element_type=jnp.float32
        )
        masked = amp_ref[pair] * full.astype(jnp.bfloat16)
        for d in range(D):
            x, z = divmod(d, ZH)
            to = jnp.where(zh == z, x * W, lax.rem(x + X - here, X) * W + NV // 2)
            out_ref[pair, :, lanes(to, W)] = masked[:, d * W : (d + 1) * W]


def chip_kernel(place_ref, mine_ref, got_ref, spread_ref, piece_ref):
    core, odd = place_ref[1], place_ref[3]
    for block_ref, number in ((mine_ref, core), (got_ref, 1 - core)):
        rows = lanes(number * ROWS, ROWS)
        for x in range(X):
            spread_ref[x, rows, :] = block_ref[...]
        piece_ref[rows, :] = block_ref[:, lanes(odd * (N // 2), N // 2)]


def trade_kernel(place_ref, crossed_ref, traded_ref, near_ref, out_ref):
    odd = place_ref[3]
    out_ref[:, lanes(odd * (N // 2), N // 2)] = crossed_ref[...]
    out_ref[:, lanes((1 - odd) * (N // 2), N // 2)] = traded_ref[...]


def far_kernel(*refs):
    for dx in range(X):
        refs[-1][dx] = refs[dx][...]


def products(mine_ref, theirs_ref, refs):
    rows = jnp.concatenate([mine_ref[0], mine_ref[1], theirs_ref[0], theirs_ref[1]], axis=0)
    for at in range(0, N, STEP):
        blocks = [r[x, :, at : at + STEP] for r in refs[:2] for x in range(X)]
        yield at, jnp.dot(rows, jnp.concatenate(blocks, axis=0), preferred_element_type=jnp.float32)


def flip_kernel(place_ref, mine_ref, theirs_ref, *refs):
    core, out_ref = place_ref[1], refs[-1]
    for column, found in products(mine_ref, theirs_ref, refs):
        turned = found.T.astype(jnp.bfloat16)
        for k in range(STEP // ROWS):
            block = turned[k * ROWS : (k + 1) * ROWS]
            for pair in range(2):
                for source in range(2):
                    start = (2 * source + pair) * ROWS
                    to = jnp.where(core == source, 0, ROWS)
                    out_ref[column // ROWS + k, pair, :, lanes(to, ROWS)] = block[:, start : start + ROWS]


def own_kernel(place_ref, mine_ref, theirs_ref, *refs):
    keep_ref, send_ref = refs[-2:]
    for column, found in products(mine_ref, theirs_ref, refs):
        found = found.astype(jnp.bfloat16)
        for pair in range(2):
            keep_ref[pair, :, column : column + STEP] = found[pair * ROWS : (pair + 1) * ROWS]
            send_ref[pair, :, column : column + STEP] = found[(2 + pair) * ROWS : (3 + pair) * ROWS]


def sum_kernel(place_ref, keep_ref, got_ref, flips_ref, out_ref):
    core = place_ref[1]
    for d in range(D):
        for number, straight_ref in enumerate((keep_ref, got_ref)):
            at = jnp.where(core == number, 0, ROWS)
            turned = flips_ref[d, 0, :, lanes(at, ROWS)].astype(jnp.float32)
            straight = straight_ref[0, :, d * ROWS : (d + 1) * ROWS].astype(jnp.float32)
            out_ref[0, :, lanes(d * W + at, ROWS)] = (straight + turned).astype(jnp.bfloat16)


def symmetrized(place, keep, got, flips):
    straight = pl.BlockSpec((1, ROWS, N), lambda i: (i, 0, 0))
    return pl.pallas_call(
        sum_kernel,
        grid=(2,),
        out_shape=shaped(2, ROWS, NV),
        in_specs=[SMEM, straight, straight, pl.BlockSpec((D, 1, ROWS, W), lambda i: (0, i, 0, 0))],
        out_specs=pl.BlockSpec((1, ROWS, NV), lambda i: (i, 0, 0)),
        compiler_params=pltpu.CompilerParams(vmem_limit_bytes=LIMIT),
        cost_estimate=pl.CostEstimate(flops=0, bytes_accessed=0, transcendentals=0),
    )(place, keep, got, flips)


def swap(array, axis, size, by):
    return lax.ppermute(array, axis, [(i, (i + by) % size) for i in range(size)])


def over_x(spread):
    return lax.all_to_all(spread, "x", split_axis=0, concat_axis=0, tiled=True)


def local(amplitudes, tile_mask, cycle_integral):
    place = jnp.stack([lax.axis_index("zh"), lax.axis_index("c"), lax.axis_index("x"), lax.axis_index("y") % 2])
    place = place.astype(jnp.int32)
    mine, theirs = call(pick_kernel, (shaped(ROWS, N),) * 2, place, cycle_integral)
    masked = call(mask_kernel, shaped(2, ROWS, NV), place, amplitudes, tile_mask)
    got = swap(theirs, "c", C, 1)
    mirrored = swap(masked, "y", Y, Y // 2)

    spread, piece = call(chip_kernel, (shaped(X, W, N), shaped(W, N // 2)), place, mine, got)
    near = lax.all_to_all(spread, "x", split_axis=0, concat_axis=0, tiled=True)
    crossed = swap(piece, "zh", ZH, 1)
    traded = lax.ppermute(crossed, "y", [(i, i ^ 1) for i in range(Y)])
    crossed = call(trade_kernel, shaped(W, N), place, crossed, traded, near, flops=0 * 10**9)
    far = [crossed] + [swap(crossed, "x", X, -d) for d in range(1, X)]
    far = call(far_kernel, shaped(X, W, N), *far, flops=15 * 10**9)
    mirrored_pair = swap(mirrored, "c", C, 1)
    masked_pair = swap(masked, "c", C, 1)
    out = call(flip_kernel, shaped(D, 2, ROWS, W), place, mirrored, mirrored_pair, near, far)
    flips = lax.all_to_all(out, ("x", "zh"), split_axis=0, concat_axis=0, tiled=True)
    keep, send = call(own_kernel, (shaped(2, ROWS, N),) * 2, place, masked, masked_pair, near, far)
    got = swap(send, "c", C, 1)
    return symmetrized(place, keep, got, flips)


def solution(mesh):
    split = Mesh(mesh.devices.reshape(Y, ZL, X, ZH, C), ("y", "zl", "x", "zh", "c"))
    pair, virt = ("y", "zl"), ("x", "zh", "c")
    return jax.shard_map(
        local,
        mesh=split,
        in_specs=(P(pair, virt, None), P(pair, virt, None), P(virt, None)),
        out_specs=P(pair, virt, None),
        check_vma=False,
    )
```

```python
import functools

import jax
import jax.numpy as jnp
from jax import lax
from jax.experimental import pallas as pl
from jax.experimental.pallas import tpu as pltpu
from jax.sharding import Mesh, PartitionSpec as P

TILE = 64
X, ZH, C, Y, ZL = 4, 2, 2, 8, 6
D = X * ZH
ROWS = 128
W = C * ROWS
NV = D * W
N = D * ROWS
HALF = N // 2
STEP = 256

VMEM = pl.BlockSpec(memory_space=pltpu.VMEM)
SMEM = pl.BlockSpec(memory_space=pltpu.SMEM)
LIMIT = 16 * 1024 * 1024


def call(kernel, out_shape, *operands, flops=0):
    many = isinstance(out_shape, tuple)
    first = SMEM if operands[0].ndim == 1 else VMEM
    return pl.pallas_call(
        kernel,
        out_shape=out_shape,
        in_specs=[first] + [VMEM] * (len(operands) - 1),
        out_specs=(VMEM,) * len(out_shape) if many else VMEM,
        compiler_params=pltpu.CompilerParams(vmem_limit_bytes=LIMIT),
        cost_estimate=pl.CostEstimate(flops=flops, bytes_accessed=0, transcendentals=0),
    )(*operands)


def shaped(*shape):
    return jax.ShapeDtypeStruct(shape, jnp.bfloat16)


def lanes(start, size):
    return pl.ds(pl.multiple_of(start, ROWS), size)


def pick_kernel(place_ref, x_ref, mine_ref, theirs_ref):
    core = place_ref[1]
    for out_ref, number in ((mine_ref, core), (theirs_ref, 1 - core)):
        for d in range(D):
            out_ref[:, d * ROWS : (d + 1) * ROWS] = x_ref[:, lanes(d * W + number * ROWS, ROWS)]


def mask_kernel(place_ref, amp_ref, mask_ref, out_ref):
    zh, here = place_ref[0], place_ref[2]
    blocks, tiles = mask_ref.shape[1:]
    spread = (
        lax.broadcasted_iota(jnp.int32, (tiles, NV), 1) // TILE
        == lax.broadcasted_iota(jnp.int32, (tiles, NV), 0)
    ).astype(jnp.bfloat16)
    for pair in range(2):
        rows = [
            jnp.broadcast_to(mask_ref[pair, b : b + 1, :].astype(jnp.float32), (TILE, tiles))
            for b in range(blocks)
        ]
        full = jnp.dot(
            jnp.concatenate(rows, axis=0).astype(jnp.bfloat16), spread, preferred_element_type=jnp.float32
        )
        masked = amp_ref[pair] * full.astype(jnp.bfloat16)
        for d in range(D):
            x, z = divmod(d, ZH)
            to = jnp.where(zh == z, x * W, lax.rem(x + X - here, X) * W + NV // 2)
            out_ref[pair, :, lanes(to, W)] = masked[:, d * W : (d + 1) * W]


def chip_kernel(place_ref, mine_ref, got_ref, spread_ref, *part_refs):
    core = place_ref[1]
    for block_ref, number in ((mine_ref, core), (got_ref, 1 - core)):
        rows = lanes(number * ROWS, ROWS)
        for x in range(X):
            spread_ref[x, rows, :] = block_ref[...]
        for half, part_ref in enumerate(part_refs):
            part_ref[rows, :] = block_ref[:, half * HALF : (half + 1) * HALF]


def copy_kernel(block_ref, *refs):
    refs[-1][...] = block_ref[...]


def far_kernel(*refs):
    for half in range(2):
        for dx in range(X):
            refs[-1][dx, :, half * HALF : (half + 1) * HALF] = refs[half * X + dx][...]


def products(mine_ref, theirs_ref, refs):
    rows = jnp.concatenate([mine_ref[0], mine_ref[1], theirs_ref[0], theirs_ref[1]], axis=0)
    for at in range(0, N, STEP):
        blocks = [r[x, :, at : at + STEP] for r in refs[:2] for x in range(X)]
        yield at, jnp.dot(rows, jnp.concatenate(blocks, axis=0), preferred_element_type=jnp.float32)


def flip_kernel(place_ref, mine_ref, theirs_ref, *refs):
    core, out_ref = place_ref[1], refs[-1]
    for column, found in products(mine_ref, theirs_ref, refs):
        turned = found.T.astype(jnp.bfloat16)
        for k in range(STEP // ROWS):
            block = turned[k * ROWS : (k + 1) * ROWS]
            for pair in range(2):
                for source in range(2):
                    start = (2 * source + pair) * ROWS
                    to = jnp.where(core == source, 0, ROWS)
                    out_ref[column // ROWS + k, pair, :, lanes(to, ROWS)] = block[:, start : start + ROWS]


def own_kernel(place_ref, mine_ref, theirs_ref, *refs):
    keep_ref, send_ref = refs[-2:]
    for column, found in products(mine_ref, theirs_ref, refs):
        found = found.astype(jnp.bfloat16)
        for pair in range(2):
            keep_ref[pair, :, column : column + STEP] = found[pair * ROWS : (pair + 1) * ROWS]
            send_ref[pair, :, column : column + STEP] = found[(2 + pair) * ROWS : (3 + pair) * ROWS]


def sum_kernel(place_ref, keep_ref, got_ref, flips_ref, out_ref):
    core = place_ref[1]
    for d in range(D):
        for number, straight_ref in enumerate((keep_ref, got_ref)):
            at = jnp.where(core == number, 0, ROWS)
            turned = flips_ref[d, 0, :, lanes(at, ROWS)].astype(jnp.float32)
            straight = straight_ref[0, :, d * ROWS : (d + 1) * ROWS].astype(jnp.float32)
            out_ref[0, :, lanes(d * W + at, ROWS)] = (straight + turned).astype(jnp.bfloat16)


def symmetrized(place, keep, got, flips):
    straight = pl.BlockSpec((1, ROWS, N), lambda i: (i, 0, 0))
    return pl.pallas_call(
        sum_kernel,
        grid=(2,),
        out_shape=shaped(2, ROWS, NV),
        in_specs=[SMEM, straight, straight, pl.BlockSpec((D, 1, ROWS, W), lambda i: (0, i, 0, 0))],
        out_specs=pl.BlockSpec((1, ROWS, NV), lambda i: (i, 0, 0)),
        compiler_params=pltpu.CompilerParams(vmem_limit_bytes=LIMIT),
        cost_estimate=pl.CostEstimate(flops=0, bytes_accessed=0, transcendentals=0),
    )(place, keep, got, flips)


def swap(array, axis, size, by):
    return lax.ppermute(array, axis, [(i, (i + by) % size) for i in range(size)])


def over_x(spread):
    return lax.all_to_all(spread, "x", split_axis=0, concat_axis=0, tiled=True)


def local(amplitudes, tile_mask, cycle_integral):
    place = jnp.stack([lax.axis_index("zh"), lax.axis_index("c"), lax.axis_index("x")])
    place = place.astype(jnp.int32)
    mine, theirs = call(pick_kernel, (shaped(ROWS, N),) * 2, place, cycle_integral)
    masked = call(mask_kernel, shaped(2, ROWS, NV), place, amplitudes, tile_mask)
    got = swap(theirs, "c", C, 1)
    mirrored = swap(masked, "y", Y, Y // 2)

    half = shaped(W, HALF)
    spread, *parts = call(chip_kernel, (shaped(X, W, N), half, half), place, mine, got)
    near = lax.all_to_all(spread, "x", split_axis=0, concat_axis=0, tiled=True)
    crossed = [call(copy_kernel, half, swap(part, "zh", ZH, 1), flops=12 * 10**9) for part in parts]
    crossed[1] = call(copy_kernel, half, crossed[1], near)
    far = []
    for block in crossed:
        far += [block] + [swap(block, "x", X, -d) for d in range(1, X)]
    far = call(far_kernel, shaped(X, W, N), *far, flops=10 * 10**9)
    mirrored_pair = swap(mirrored, "c", C, 1)
    masked_pair = swap(masked, "c", C, 1)
    out = call(flip_kernel, shaped(D, 2, ROWS, W), place, mirrored, mirrored_pair, near, far)
    flips = lax.all_to_all(out, ("x", "zh"), split_axis=0, concat_axis=0, tiled=True)
    keep, send = call(own_kernel, (shaped(2, ROWS, N),) * 2, place, masked, masked_pair, near, far)
    got = swap(send, "c", C, 1)
    return symmetrized(place, keep, got, flips)


def solution(mesh):
    split = Mesh(mesh.devices.reshape(Y, ZL, X, ZH, C), ("y", "zl", "x", "zh", "c"))
    pair, virt = ("y", "zl"), ("x", "zh", "c")
    return jax.shard_map(
        local,
        mesh=split,
        in_specs=(P(pair, virt, None), P(pair, virt, None), P(virt, None)),
        out_specs=P(pair, virt, None),
        check_vma=False,
    )
```

```python
import functools

import jax
import jax.numpy as jnp
from jax import lax
from jax.experimental import pallas as pl
from jax.experimental.pallas import tpu as pltpu
from jax.sharding import Mesh, PartitionSpec as P

TILE = 64
X, ZH, C, Y, ZL = 4, 2, 2, 8, 6
D = X * ZH
ROWS = 128
W = C * ROWS
NV = D * W
N = D * ROWS
HALF = N // 2
STEP = 256

VMEM = pl.BlockSpec(memory_space=pltpu.VMEM)
SMEM = pl.BlockSpec(memory_space=pltpu.SMEM)
LIMIT = 16 * 1024 * 1024


def call(kernel, out_shape, *operands, flops=0):
    many = isinstance(out_shape, tuple)
    first = SMEM if operands[0].ndim == 1 else VMEM
    return pl.pallas_call(
        kernel,
        out_shape=out_shape,
        in_specs=[first] + [VMEM] * (len(operands) - 1),
        out_specs=(VMEM,) * len(out_shape) if many else VMEM,
        compiler_params=pltpu.CompilerParams(vmem_limit_bytes=LIMIT),
        cost_estimate=pl.CostEstimate(flops=flops, bytes_accessed=0, transcendentals=0),
    )(*operands)


def shaped(*shape):
    return jax.ShapeDtypeStruct(shape, jnp.bfloat16)


def lanes(start, size):
    return pl.ds(pl.multiple_of(start, ROWS), size)


def pick(core, x_ref, mine_ref, theirs_ref):
    for out_ref, number in ((mine_ref, core), (theirs_ref, 1 - core)):
        for d in range(D):
            out_ref[:, d * ROWS : (d + 1) * ROWS] = x_ref[:, lanes(d * W + number * ROWS, ROWS)]


def first_kernel(place_ref, x_ref, amp_ref, mask_ref, mine_ref, theirs_ref, out_ref):
    pick(place_ref[1], x_ref, mine_ref, theirs_ref)
    zh, here = place_ref[0], place_ref[2]
    blocks, tiles = mask_ref.shape[1:]
    spread = (
        lax.broadcasted_iota(jnp.int32, (tiles, NV), 1) // TILE
        == lax.broadcasted_iota(jnp.int32, (tiles, NV), 0)
    ).astype(jnp.bfloat16)
    for pair in range(2):
        rows = [
            jnp.broadcast_to(mask_ref[pair, b : b + 1, :].astype(jnp.float32), (TILE, tiles))
            for b in range(blocks)
        ]
        full = jnp.dot(
            jnp.concatenate(rows, axis=0).astype(jnp.bfloat16), spread, preferred_element_type=jnp.float32
        )
        masked = amp_ref[pair] * full.astype(jnp.bfloat16)
        for d in range(D):
            x, z = divmod(d, ZH)
            to = jnp.where(zh == z, x * W, lax.rem(x + X - here, X) * W + NV // 2)
            out_ref[pair, :, lanes(to, W)] = masked[:, d * W : (d + 1) * W]


def chip_kernel(place_ref, mine_ref, got_ref, spread_ref, *part_refs):
    core = place_ref[1]
    for block_ref, number in ((mine_ref, core), (got_ref, 1 - core)):
        rows = lanes(number * ROWS, ROWS)
        for x in range(X):
            spread_ref[x, rows, :] = block_ref[...]
        for half, part_ref in enumerate(part_refs):
            part_ref[rows, :] = block_ref[:, half * HALF : (half + 1) * HALF]


def copy_kernel(block_ref, *refs):
    refs[-1][...] = block_ref[...]


def far_kernel(*refs):
    for half in range(2):
        for dx in range(X):
            refs[-1][dx, :, half * HALF : (half + 1) * HALF] = refs[half * X + dx][...]


def products(mine_ref, theirs_ref, refs):
    rows = jnp.concatenate([mine_ref[0], mine_ref[1], theirs_ref[0], theirs_ref[1]], axis=0)
    for at in range(0, N, STEP):
        blocks = [r[x, :, at : at + STEP] for r in refs[:2] for x in range(X)]
        yield at, jnp.dot(rows, jnp.concatenate(blocks, axis=0), preferred_element_type=jnp.float32)


def flip_kernel(place_ref, mine_ref, theirs_ref, *refs):
    core, out_ref = place_ref[1], refs[-1]
    for column, found in products(mine_ref, theirs_ref, refs):
        turned = found.T.astype(jnp.bfloat16)
        for k in range(STEP // ROWS):
            block = turned[k * ROWS : (k + 1) * ROWS]
            for pair in range(2):
                for source in range(2):
                    start = (2 * source + pair) * ROWS
                    to = jnp.where(core == source, 0, ROWS)
                    out_ref[column // ROWS + k, pair, :, lanes(to, ROWS)] = block[:, start : start + ROWS]


def own_kernel(place_ref, mine_ref, theirs_ref, *refs):
    keep_ref, send_ref = refs[-2:]
    for column, found in products(mine_ref, theirs_ref, refs):
        found = found.astype(jnp.bfloat16)
        for pair in range(2):
            keep_ref[pair, :, column : column + STEP] = found[pair * ROWS : (pair + 1) * ROWS]
            send_ref[pair, :, column : column + STEP] = found[(2 + pair) * ROWS : (3 + pair) * ROWS]


def sum_kernel(place_ref, keep_ref, got_ref, flips_ref, out_ref):
    core = place_ref[1]
    for d in range(D):
        for number, straight_ref in enumerate((keep_ref, got_ref)):
            at = jnp.where(core == number, 0, ROWS)
            turned = flips_ref[d, 0, :, lanes(at, ROWS)].astype(jnp.float32)
            straight = straight_ref[0, :, d * ROWS : (d + 1) * ROWS].astype(jnp.float32)
            out_ref[0, :, lanes(d * W + at, ROWS)] = (straight + turned).astype(jnp.bfloat16)


def symmetrized(place, keep, got, flips):
    straight = pl.BlockSpec((1, ROWS, N), lambda i: (i, 0, 0))
    return pl.pallas_call(
        sum_kernel,
        grid=(2,),
        out_shape=shaped(2, ROWS, NV),
        in_specs=[SMEM, straight, straight, pl.BlockSpec((D, 1, ROWS, W), lambda i: (0, i, 0, 0))],
        out_specs=pl.BlockSpec((1, ROWS, NV), lambda i: (i, 0, 0)),
        compiler_params=pltpu.CompilerParams(vmem_limit_bytes=LIMIT),
        cost_estimate=pl.CostEstimate(flops=0, bytes_accessed=0, transcendentals=0),
    )(place, keep, got, flips)


def swap(array, axis, size, by):
    return lax.ppermute(array, axis, [(i, (i + by) % size) for i in range(size)])


def over_x(spread):
    return lax.all_to_all(spread, "x", split_axis=0, concat_axis=0, tiled=True)


def local(amplitudes, tile_mask, cycle_integral):
    place = jnp.stack([lax.axis_index("zh"), lax.axis_index("c"), lax.axis_index("x")])
    place = place.astype(jnp.int32)
    outs = (shaped(ROWS, N), shaped(ROWS, N), shaped(2, ROWS, NV))
    mine, theirs, masked = call(first_kernel, outs, place, cycle_integral, amplitudes, tile_mask)
    got = swap(theirs, "c", C, 1)
    mirrored = swap(masked, "y", Y, Y // 2)

    half = shaped(W, HALF)
    spread, *parts = call(chip_kernel, (shaped(X, W, N), half, half), place, mine, got)
    near = lax.all_to_all(spread, "x", split_axis=0, concat_axis=0, tiled=True)
    crossed = [call(copy_kernel, half, swap(part, "zh", ZH, 1), flops=6 * 10**9) for part in parts]
    crossed[1] = call(copy_kernel, half, crossed[1], near)
    far = []
    for block in crossed:
        far += [block] + [swap(block, "x", X, -d) for d in range(1, X)]
    far = call(far_kernel, shaped(X, W, N), *far, flops=10 * 10**9)
    mirrored_pair = swap(mirrored, "c", C, 1)
    masked_pair = swap(masked, "c", C, 1)
    out = call(flip_kernel, shaped(D, 2, ROWS, W), place, mirrored, mirrored_pair, near, far)
    flips = lax.all_to_all(out, ("x", "zh"), split_axis=0, concat_axis=0, tiled=True)
    keep, send = call(own_kernel, (shaped(2, ROWS, N),) * 2, place, masked, masked_pair, near, far)
    got = swap(send, "c", C, 1)
    return symmetrized(place, keep, got, flips)


def solution(mesh):
    split = Mesh(mesh.devices.reshape(Y, ZL, X, ZH, C), ("y", "zl", "x", "zh", "c"))
    pair, virt = ("y", "zl"), ("x", "zh", "c")
    return jax.shard_map(
        local,
        mesh=split,
        in_specs=(P(pair, virt, None), P(pair, virt, None), P(virt, None)),
        out_specs=P(pair, virt, None),
        check_vma=False,
    )
```
